32 devices in a mesh: groups: 2 (over x), row: 4 (over y, core), col: 4 (over z).
Axes of the slice: x: 2, y: 2, z: 4, core: 2. Of those that a mesh axis runs over, the one named last changes fastest.
Arguments:
- embedding: bfloat16 [1024, 64, 128], P(('groups', 'row', 'col')), parts along dimension 0, may hold values from -6 to 6
- combined: float32 [1024, 64, 128], P(('groups', 'col', 'row')), parts along dimension 0, may hold values from -6 to 6
- blocks: bfloat16 [32, 256, 128, 128], P(('groups', 'row', 'col')), parts along dimension 0, may hold values from 0 to 1
- block_rows: int32 [32, 256], P(('groups', 'row', 'col')), parts along dimension 0, may hold values from 0 to 127
- block_cols: int32 [32, 256], P(('groups', 'row', 'col')), parts along dimension 0, may hold values from 0 to 127, as said below
- block_counts: int32 [32], P(('groups', 'row', 'col')), parts along dimension 0, may hold values from 64 to 256, as said below
- degrees: int32 [131072], P('groups'), parts along dimension 0, may hold values from 8 to 128
Outputs:
- next_layer: bfloat16 [1024, 64, 128], P(('groups', 'col', 'row')), parts along dimension 0
- combined_out: float32 [1024, 64, 128], P(('groups', 'col', 'row')), parts along dimension 0
The draws below stay inside these ranges and needn't reach their ends.
There are 2 independent parts, one for each index of `groups`. The reference program is written for one: setup_inputs(seed, part) draws one part's arguments, and reference() takes and returns one part's arrays. A program takes and returns all parts, laid end to end along the dimension named above; each array names one. Nothing has to cross between parts.
Inputs may be any that keep to these rules, and one draw needn't show every extreme that they name: `block_counts`: some tile's list holds exactly 256 live blocks. `block_cols`: in each tile's list, at most 64 slots (live or not) name block columns of one share s, the columns s * 32 to (s + 1) * 32 - 1, and in every tile some share is named by exactly 64 slots.
All inputs are finite; a program needn't handle non-finite values.
Results may differ from the reference program's by a relative error of at most 0.0049.
Values may be sent and summed in bfloat16 or wider, within the bound.
A program may use at most 128 MiB of HBM per device.

```python
import jax
import jax.numpy as jnp
from jax import lax

W = 64
BLK = 128
MAXB = 256
NB = 512
RB = 128
CB = 128
N_ROW = 4
N_COL = 4


def draw_block_counts(key, part):
    key = jax.random.fold_in(key, 5)
    first_key, second_key = jax.random.split(key)
    tile_total = N_ROW * N_COL
    drawn = jax.random.randint(first_key, (tile_total,), max(1, MAXB // 4), MAXB + 1, dtype=jnp.int32)
    chosen = jax.random.randint(second_key, (), 0, tile_total, dtype=jnp.int32)
    return jnp.where(jnp.arange(tile_total, dtype=jnp.int32) == chosen, jnp.int32(MAXB), drawn)


def draw_block_cols(key, part):
    key = jax.random.fold_in(key, 7)
    first_key, second_key = jax.random.split(key)
    tile_total = N_ROW * N_COL
    share_cap = max(1, MAXB // N_ROW)
    share_width = CB // N_ROW
    pool = jnp.arange(N_ROW * share_cap, dtype=jnp.int32) // share_cap
    tile_keys = jax.random.split(first_key, tile_total)
    owners = jax.vmap(lambda k: jax.random.permutation(k, pool)[:MAXB])(tile_keys)
    within = jax.random.randint(second_key, (tile_total, MAXB), 0, share_width, dtype=jnp.int32)
    return (owners * share_width + within).astype(jnp.int32)


def place_ends(result, own_key, smallest, top_value):
    extent = result.shape
    place = [jax.random.randint(jax.random.fold_in(own_key, axis), (), 0, extent[axis]) for axis in range(len(extent))]
    result = result.at[tuple(place)].set(smallest)
    longest = extent.index(max(extent))
    place[longest] = (place[longest] + 1) % extent[longest]
    return result.at[tuple(place)].set(top_value)


def block_levels(stream_key, extent, shards, smallest, high):
    gain, own = 1.0, jax.random.fold_in(stream_key, 6)
    for axis_at, shards_of in shards:
        steps = jnp.exp(jax.random.uniform(jax.random.fold_in(own, axis_at), (shards_of,), jnp.float32, smallest / len(shards), high / len(shards)))
        gain = gain * jnp.repeat(steps, extent[axis_at] // shards_of).reshape([-1 if axis == axis_at else 1 for axis in range(len(extent))])
    return gain


def noise(own_key, extent, spread, reach, pieces=(), held_as=jnp.bfloat16):
    gain = block_levels(own_key, extent, pieces, -0.22, 0.18) if pieces else 1.0
    result = jax.random.normal(own_key, extent, jnp.float32) * spread * gain
    return jnp.minimum(jnp.maximum(result, -reach), reach).astype(held_as)


def setup_inputs(seed: int = 0, part: int = 0) -> dict:
    key_list = jax.random.split(jax.random.key(seed), 8)
    part_splits = jax.random.split(jax.random.fold_in(key_list[7], part), 8)
    embedding = noise(part_splits[0], (NB, W, BLK), 1.0, 6.0, ((0, 16),))
    combined = noise(part_splits[1], (NB, W, BLK), 1.0, 6.0, ((0, 16),), jnp.float32)
    blocks = jnp.clip(1.0 * jax.random.uniform(part_splits[2], (N_ROW * N_COL, MAXB, BLK, BLK), jnp.float32) ** block_levels(part_splits[2], (N_ROW * N_COL, MAXB, BLK, BLK), ((0, 16),), -0.2, 0.2), 0.0, 1.0).astype(jnp.bfloat16)
    block_rows = place_ends(jax.random.randint(part_splits[3], (N_ROW * N_COL, MAXB), 0, RB), jax.random.fold_in(part_splits[3], 1), 0, RB - 1).astype(jnp.int32)
    block_cols = draw_block_cols(jax.random.fold_in(jax.random.fold_in(key_list[7], part), 71), part)
    block_counts = draw_block_counts(jax.random.fold_in(jax.random.fold_in(key_list[7], part), 71), part)
    degrees = place_ends(jax.random.randint(part_splits[6], (NB * BLK,), 8, 129), jax.random.fold_in(part_splits[6], 1), 8, 128).astype(jnp.int32)
    return dict(embedding=embedding, combined=combined, blocks=blocks, block_rows=block_rows, block_cols=block_cols, block_counts=block_counts, degrees=degrees)


def reference(embedding, combined, blocks, block_rows, block_cols, block_counts, degrees):
    node_blocks = embedding.shape[0]
    lane_count = embedding.shape[2]
    row_span = node_blocks // N_ROW
    col_span = node_blocks // N_COL
    inv_root = (1.0 / jnp.sqrt(degrees.astype(jnp.float32))).reshape(node_blocks, 1, lane_count)
    scaled = (embedding.astype(jnp.float32) * inv_root).astype(jnp.bfloat16)
    slot_ids = jnp.arange(MAXB, dtype=jnp.int32)

    def tile_step(total, tile_index):
        row_part = tile_index // N_COL
        col_part = tile_index % N_COL
        picked = scaled[row_part * row_span + block_rows[tile_index]]
        products = jnp.einsum('kwr,krc->kwc', picked.astype(jnp.float32), blocks[tile_index].astype(jnp.float32))
        alive_mask = (slot_ids < block_counts[tile_index])[:, None, None]
        products = jnp.where(alive_mask, products, jnp.zeros_like(products))
        return (total.at[col_part * col_span + block_cols[tile_index]].add(products), None)
    total, _ = lax.scan(tile_step, jnp.zeros(embedding.shape, jnp.float32), jnp.arange(N_ROW * N_COL, dtype=jnp.int32))
    update = total * inv_root
    return (update.astype(jnp.bfloat16), combined + update)
```

```python
import functools

import jax
import jax.numpy as jnp
from jax import lax
from jax.experimental import pallas as pl
from jax.experimental.pallas import tpu as pltpu
from jax.sharding import PartitionSpec as P

MESH = pl.DeviceIdType.MESH
FEATS = 16
PIECES = 4


def layer_kernel(
    n_row,
    n_col,
    emb_ref,
    scale_ref,
    blocks_ref,
    perm_ref,
    src_ref,
    keep_ref,
    alive_ref,
    last_ref,
    full_ref,
    out_ref,
    tiles,
    gath,
    part,
    recv,
    running,
    blk_sem,
    ag_send,
    ag_recv,
    fw_send,
    rs_send,
    rs_recv,
):
    own = emb_ref.shape[0]
    chunks = emb_ref.shape[1] // FEATS
    slots = blocks_ref.shape[0]
    per_share = slots // n_row
    piece = slots // PIECES
    g = lax.axis_index("groups")
    r = lax.axis_index("row")
    c = lax.axis_index("col")

    def block_copy(i):
        span = pl.ds(i * piece, piece)
        return pltpu.make_async_copy(blocks_ref.at[span], tiles.at[span], blk_sem.at[i])

    for i in range(PIECES):
        block_copy(i).start()

    def row_peer(j):
        base = lax.rem(r + (j - j % 2), n_row)
        return base if j % 2 == 0 else base + 1 - 2 * lax.rem(base, 2)

    barrier = pltpu.get_barrier_semaphore()
    for d in range(1, n_col):
        pl.semaphore_signal(
            barrier, inc=1, device_id=(g, r, lax.rem(c + d, n_col)), device_id_type=MESH
        )
    for j in range(1, n_row):
        pl.semaphore_signal(barrier, inc=1, device_id=(g, row_peer(j), c), device_id_type=MESH)

    def scale_chunk(ch):
        feats = pl.ds(ch * FEATS, FEATS)
        gath[ch][pl.ds(c * own, own)] = (
            emb_ref[:, feats, :].astype(jnp.float32) * scale_ref[...]
        ).astype(jnp.bfloat16)

    for ch in range(chunks):
        scale_chunk(ch)
    pl.semaphore_wait(barrier, n_col - 1 + n_row - 1)

    def shard_copy(ch, shard, send, target):
        span = gath[ch].at[pl.ds(shard * own, own)]
        return pltpu.make_async_remote_copy(
            src_ref=span,
            dst_ref=span,
            send_sem=send,
            recv_sem=ag_recv.at[ch, shard],
            device_id=(g, r, target),
            device_id_type=MESH,
        )

    line = n_col == 4
    if line:
        near = c + 1 - 2 * lax.rem(c, 2)
        far = lax.rem(c + 2, 4)
        across = 3 - c
        inner = jnp.logical_or(c == 1, c == 2)

    def start_own(ch):
        if line:
            shard_copy(ch, c, ag_send.at[ch, 0], far).start()
            shard_copy(ch, c, ag_send.at[ch, 1], near).start()

            @pl.when(inner)
            def _():
                shard_copy(ch, c, ag_send.at[ch, 2], across).start()
        else:
            for d in range(1, n_col):
                shard_copy(ch, c, ag_send.at[ch, d - 1], lax.rem(c + d, n_col)).start()

    def await_shards(ch):
        if line:
            shard_copy(ch, far, fw_send.at[ch], near).wait_recv()

            @pl.when(inner)
            def _():
                shard_copy(ch, far, fw_send.at[ch], near).start()

    def await_rest(ch):
        if line:
            shard_copy(ch, near, fw_send.at[ch], near).wait_recv()
            shard_copy(ch, across, fw_send.at[ch], near).wait_recv()
        else:
            for d in range(1, n_col):
                shard = lax.rem(c + d, n_col)
                shard_copy(ch, shard, ag_send.at[ch, 0], shard).wait_recv()

    def finish_sends(ch):
        if line:
            shard_copy(ch, c, ag_send.at[ch, 0], far).wait_send()
            shard_copy(ch, c, ag_send.at[ch, 1], near).wait_send()

            @pl.when(inner)
            def _():
                shard_copy(ch, c, ag_send.at[ch, 2], across).wait_send()
                shard_copy(ch, far, fw_send.at[ch], near).wait_send()
        else:
            for d in range(1, n_col):
                shard_copy(ch, c, ag_send.at[ch, d - 1], lax.rem(c + d, n_col)).wait_send()

    def sum_copy(ch, j):
        return pltpu.make_async_remote_copy(
            src_ref=part.at[ch, j],
            dst_ref=recv.at[ch, j],
            send_sem=rs_send.at[ch, j],
            recv_sem=rs_recv.at[ch, j],
            device_id=(g, row_peer(j), c),
            device_id_type=MESH,
        )

    def share_sums(ch, share):
        base = share * per_share

        def slot(k, total):
            i = base + k
            x = gath[ch][src_ref[i]]
            product = jnp.dot(x, tiles[perm_ref[i]], preferred_element_type=jnp.float32)
            total = total * keep_ref[i] + product * alive_ref[i]
            running[k] = total
            return total

        lax.fori_loop(
            0, per_share, slot, jnp.zeros((FEATS, running.shape[2]), jnp.float32), unroll=16
        )

    def compute(ch):
        for j in list(range(2, n_row)) + [1, 0]:
            share = row_peer(j)
            share_sums(ch, share)

            def place(d, carry):
                i = share * own + d
                value = running[last_ref[i]] * full_ref[i]
                if j == 0:
                    out_ref[d, pl.ds(ch * FEATS, FEATS), :] = value
                else:
                    part[ch, j, d] = value.astype(jnp.bfloat16)
                return carry

            lax.fori_loop(0, own, place, 0, unroll=8)
            if j:
                sum_copy(ch, j).start()

    def reduce(ch):
        feats = pl.ds(ch * FEATS, FEATS)
        for j in range(1, n_row):
            sum_copy(ch, j).wait_recv()
        value = out_ref[:, feats, :]
        for j in range(1, n_row):
            value = value + recv[ch, j].astype(jnp.float32)
        out_ref[:, feats, :] = value

    start_own(0)
    start_own(1)
    for i in range(PIECES):
        block_copy(i).wait()
    for ch in range(chunks):
        await_shards(ch)
        if ch + 2 < chunks:
            start_own(ch + 2)
        await_rest(ch)
        compute(ch)
        if ch:
            reduce(ch - 1)
    reduce(chunks - 1)
    for ch in range(chunks):
        finish_sends(ch)
        for j in range(1, n_row):
            sum_copy(ch, j).wait_send()


def propagate(n_row, n_col, emb, scale, tiles, perm, src, keep, alive, last, full):
    own, width, lanes = emb.shape
    slots = tiles.shape[0]
    chunks = width // FEATS
    vmem = pl.BlockSpec(memory_space=pltpu.VMEM)
    smem = pl.BlockSpec(memory_space=pltpu.SMEM)
    return pl.pallas_call(
        functools.partial(layer_kernel, n_row, n_col),
        out_shape=jax.ShapeDtypeStruct((own, width, lanes), jnp.float32),
        in_specs=[vmem, vmem, pl.BlockSpec(memory_space=pl.ANY)] + [smem] * 6,
        out_specs=vmem,
        scratch_shapes=[
            pltpu.VMEM((slots, lanes, lanes), jnp.bfloat16),
            [pltpu.VMEM((n_col * own, FEATS, lanes), jnp.bfloat16) for _ in range(chunks)],
            pltpu.VMEM((chunks, n_row, own, FEATS, lanes), jnp.bfloat16),
            pltpu.VMEM((chunks, n_row, own, FEATS, lanes), jnp.bfloat16),
            pltpu.VMEM((slots // n_row, FEATS, lanes), jnp.float32),
            pltpu.SemaphoreType.DMA((PIECES,)),
            pltpu.SemaphoreType.DMA((chunks, n_col)),
            pltpu.SemaphoreType.DMA((chunks, n_col)),
            pltpu.SemaphoreType.DMA((chunks,)),
            pltpu.SemaphoreType.DMA((chunks, n_row)),
            pltpu.SemaphoreType.DMA((chunks, n_row)),
        ],
        compiler_params=pltpu.CompilerParams(
            collective_id=0, has_side_effects=True, vmem_limit_bytes=48 * 1024 * 1024
        ),
    )(emb, scale, tiles, perm, src, keep, alive, last, full)


def slot_order(rows, cols, count, n_row, own):
    slots = rows.shape[0]
    ids = jnp.arange(slots, dtype=jnp.int32)
    key = cols * slots + ids
    rank = jnp.sum((key[None, :] < key[:, None]).astype(jnp.int32), axis=1)
    hit = rank[None, :] == ids[:, None]

    def ordered(values):
        return jnp.sum(jnp.where(hit, values[None, :], 0), axis=1)

    perm = ordered(ids)
    src = ordered(rows)
    col = ordered(cols)
    alive = (perm < count).astype(jnp.float32)
    before = jnp.concatenate([jnp.full((1,), -1, jnp.int32), col[:-1]])
    keep = (before == col).astype(jnp.float32)
    dest = jnp.arange(n_row * own, dtype=jnp.int32)
    upto = jnp.sum((cols[None, :] <= dest[:, None]).astype(jnp.int32), axis=1)
    full = jnp.any(cols[None, :] == dest[:, None], axis=1).astype(jnp.float32)
    last = jnp.clip(upto - 1 - (dest // own) * (slots // n_row), 0, slots // n_row - 1)
    return perm, src, keep, alive, last, full


def shards(embedding, combined, blocks, block_rows, block_cols, block_counts, degrees):
    n_row = lax.axis_size("row")
    n_col = lax.axis_size("col")
    r = lax.axis_index("row")
    c = lax.axis_index("col")
    own, _, lanes = embedding.shape

    def root(first):
        part = lax.dynamic_slice_in_dim(degrees, first * own * lanes, own * lanes, 0)
        return (1.0 / jnp.sqrt(part.astype(jnp.float32))).reshape(own, 1, lanes)

    order = slot_order(block_rows[0], block_cols[0], block_counts[0], n_row, own)
    total = propagate(n_row, n_col, embedding, root(r * n_col + c), blocks[0], *order)
    update = total * root(c * n_row + r)
    return update.astype(jnp.bfloat16), combined + update


def solution(mesh):
    return jax.shard_map(
        shards,
        mesh=mesh,
        in_specs=(
            P(("groups", "row", "col"), None, None),
            P(("groups", "col", "row"), None, None),
            P(("groups", "row", "col"), None, None, None),
            P(("groups", "row", "col"), None),
            P(("groups", "row", "col"), None),
            P(("groups", "row", "col")),
            P("groups"),
        ),
        out_specs=(
            P(("groups", "col", "row"), None, None),
            P(("groups", "col", "row"), None, None),
        ),
        check_vma=False,
    )
```

```python
import functools

import jax
import jax.numpy as jnp
from jax import lax
from jax.experimental import pallas as pl
from jax.experimental.pallas import tpu as pltpu
from jax.sharding import PartitionSpec as P

MESH = pl.DeviceIdType.MESH
FEATS = 16
PIECES = 4


def order_slots(n_row, own, rows_ref, cols_ref, count_ref, whole, real):
    slots = rows_ref.shape[1]
    dests = n_row * own
    per_share = slots // n_row
    shape = (slots, slots)
    down = lax.broadcasted_iota(jnp.int32, shape, 0)
    along = lax.broadcasted_iota(jnp.int32, shape, 1)
    both = cols_ref[...] * slots + rows_ref[...]
    both_down = jnp.sum(jnp.where(down == along, both, 0), axis=1, keepdims=True)
    cols = cols_ref[...]
    cols_down = both_down // slots
    earlier = cols * slots + along < cols_down * slots + down
    rank = jnp.sum(earlier.astype(jnp.int32), axis=1, keepdims=True)
    same = jnp.logical_and(earlier, cols == cols_down)
    repeats = (jnp.sum(same.astype(jnp.int32), axis=1, keepdims=True) > 0).astype(jnp.float32)
    hit = rank == along
    down_one = lax.broadcasted_iota(jnp.int32, (slots, 1), 0)
    alive = (down_one < count_ref[0]).astype(jnp.float32)

    def ordered(values):
        return jnp.sum(jnp.where(hit, values, jnp.zeros_like(values)), axis=0, keepdims=True)

    whole[0:1, 0:slots] = ordered(down_one)
    whole[1:2, 0:slots] = ordered(both_down - cols_down * slots)
    real[0:1, 0:slots] = ordered(repeats)
    real[1:2, 0:slots] = ordered(alive)
    dest = lax.broadcasted_iota(jnp.int32, (slots, dests), 1)
    upto = jnp.sum((cols_down <= dest).astype(jnp.int32), axis=0, keepdims=True)
    named = jnp.sum((cols_down == dest).astype(jnp.int32), axis=0, keepdims=True)
    dest_one = lax.broadcasted_iota(jnp.int32, (1, dests), 1)
    last = upto - 1 - dest_one // own * per_share
    whole[2:3, 0:dests] = jnp.clip(last, 0, per_share - 1)
    real[2:3, 0:dests] = (named > 0).astype(jnp.float32)


def layer_kernel(
    n_row,
    n_col,
    emb_hbm,
    degree_hbm,
    blocks_ref,
    rows_ref,
    cols_ref,
    count_ref,
    out_ref,
    emb_ref,
    degree_ref,
    whole_vmem,
    real_vmem,
    whole_smem,
    real_smem,
    tiles,
    gath,
    part,
    recv,
    running,
    blk_sem,
    in_sem,
    ag_send,
    ag_recv,
    fw_send,
    rs_send,
    rs_recv,
):
    own = emb_hbm.shape[0]
    chunks = emb_hbm.shape[1] // FEATS
    slots = blocks_ref.shape[0]
    per_share = slots // n_row
    piece = slots // PIECES
    g = lax.axis_index("groups")
    r = lax.axis_index("row")
    c = lax.axis_index("col")

    def block_copy(i):
        span = pl.ds(i * piece, piece)
        return pltpu.make_async_copy(blocks_ref.at[span], tiles.at[span], blk_sem.at[i])

    first = (r * n_col + c) * own
    emb_copy = pltpu.make_async_copy(emb_hbm, emb_ref, in_sem.at[0])
    degree_copy = pltpu.make_async_copy(degree_hbm.at[pl.ds(first, own)], degree_ref, in_sem.at[1])
    emb_copy.start()
    degree_copy.start()
    for i in range(PIECES):
        block_copy(i).start()

    def row_peer(j):
        base = lax.rem(r + (j - j % 2), n_row)
        return base if j % 2 == 0 else base + 1 - 2 * lax.rem(base, 2)

    barrier = pltpu.get_barrier_semaphore()
    for d in range(1, n_col):
        pl.semaphore_signal(
            barrier, inc=1, device_id=(g, r, lax.rem(c + d, n_col)), device_id_type=MESH
        )
    for j in range(1, n_row):
        pl.semaphore_signal(barrier, inc=1, device_id=(g, row_peer(j), c), device_id_type=MESH)

    degree_copy.wait()
    emb_copy.wait()
    scale = (1.0 / jnp.sqrt(degree_ref[...].astype(jnp.float32)))[:, None, :]

    def scale_chunk(ch):
        feats = pl.ds(ch * FEATS, FEATS)
        gath[ch][pl.ds(c * own, own)] = (
            emb_ref[:, feats, :].astype(jnp.float32) * scale
        ).astype(jnp.bfloat16)

    for ch in range(chunks):
        scale_chunk(ch)
    pl.semaphore_wait(barrier, n_col - 1 + n_row - 1)

    def shard_copy(ch, shard, send, target):
        span = gath[ch].at[pl.ds(shard * own, own)]
        return pltpu.make_async_remote_copy(
            src_ref=span,
            dst_ref=span,
            send_sem=send,
            recv_sem=ag_recv.at[ch, shard],
            device_id=(g, r, target),
            device_id_type=MESH,
        )

    line = n_col == 4
    if line:
        near = c + 1 - 2 * lax.rem(c, 2)
        far = lax.rem(c + 2, 4)
        across = 3 - c
        inner = jnp.logical_or(c == 1, c == 2)

    def start_own(ch):
        if line:
            shard_copy(ch, c, ag_send.at[ch, 0], far).start()
            shard_copy(ch, c, ag_send.at[ch, 1], near).start()

            @pl.when(inner)
            def _():
                shard_copy(ch, c, ag_send.at[ch, 2], across).start()
        else:
            for d in range(1, n_col):
                shard_copy(ch, c, ag_send.at[ch, d - 1], lax.rem(c + d, n_col)).start()

    def await_shards(ch):
        if line:
            shard_copy(ch, far, fw_send.at[ch], near).wait_recv()

            @pl.when(inner)
            def _():
                shard_copy(ch, far, fw_send.at[ch], near).start()

    def await_rest(ch):
        if line:
            shard_copy(ch, near, fw_send.at[ch], near).wait_recv()
            shard_copy(ch, across, fw_send.at[ch], near).wait_recv()
        else:
            for d in range(1, n_col):
                shard = lax.rem(c + d, n_col)
                shard_copy(ch, shard, ag_send.at[ch, 0], shard).wait_recv()

    def finish_sends(ch):
        if line:
            shard_copy(ch, c, ag_send.at[ch, 0], far).wait_send()
            shard_copy(ch, c, ag_send.at[ch, 1], near).wait_send()

            @pl.when(inner)
            def _():
                shard_copy(ch, c, ag_send.at[ch, 2], across).wait_send()
                shard_copy(ch, far, fw_send.at[ch], near).wait_send()
        else:
            for d in range(1, n_col):
                shard_copy(ch, c, ag_send.at[ch, d - 1], lax.rem(c + d, n_col)).wait_send()

    def sum_copy(ch, j):
        return pltpu.make_async_remote_copy(
            src_ref=part.at[ch, j],
            dst_ref=recv.at[ch, j],
            send_sem=rs_send.at[ch, j],
            recv_sem=rs_recv.at[ch, j],
            device_id=(g, row_peer(j), c),
            device_id_type=MESH,
        )

    def share_sums(ch, share):
        base = share * per_share

        def slot(k, total):
            i = base + k
            x = gath[ch][whole_smem[1, i]]
            product = jnp.dot(x, tiles[whole_smem[0, i]], preferred_element_type=jnp.float32)
            total = total * real_smem[0, i] + product * real_smem[1, i]
            running[k] = total
            return total

        lax.fori_loop(
            0, per_share, slot, jnp.zeros((FEATS, running.shape[2]), jnp.float32), unroll=16
        )

    def compute(ch):
        for j in list(range(2, n_row)) + [1, 0]:
            share = row_peer(j)
            share_sums(ch, share)

            def place(d, carry):
                i = share * own + d
                value = running[whole_smem[2, i]] * real_smem[2, i]
                if j == 0:
                    out_ref[d, pl.ds(ch * FEATS, FEATS), :] = value
                else:
                    part[ch, j, d] = value.astype(jnp.bfloat16)
                return carry

            lax.fori_loop(0, own, place, 0, unroll=8)
            if j:
                sum_copy(ch, j).start()

    def reduce(ch):
        feats = pl.ds(ch * FEATS, FEATS)
        for j in range(1, n_row):
            sum_copy(ch, j).wait_recv()
        value = out_ref[:, feats, :]
        for j in range(1, n_row):
            value = value + recv[ch, j].astype(jnp.float32)
        out_ref[:, feats, :] = value

    start_own(0)
    start_own(1)
    order_slots(n_row, own, rows_ref, cols_ref, count_ref, whole_vmem, real_vmem)
    to_scalar = [
        pltpu.make_async_copy(whole_vmem, whole_smem, in_sem.at[2]),
        pltpu.make_async_copy(real_vmem, real_smem, in_sem.at[3]),
    ]
    for copy in to_scalar:
        copy.start()
    for copy in to_scalar:
        copy.wait()
    for i in range(PIECES):
        block_copy(i).wait()
    for ch in range(chunks):
        await_shards(ch)
        if ch + 2 < chunks:
            start_own(ch + 2)
        await_rest(ch)
        compute(ch)
        if ch:
            reduce(ch - 1)
    reduce(chunks - 1)
    for ch in range(chunks):
        finish_sends(ch)
        for j in range(1, n_row):
            sum_copy(ch, j).wait_send()


def propagate(n_row, n_col, emb, degrees, tiles, rows, cols, count):
    own, width, lanes = emb.shape
    slots = tiles.shape[0]
    chunks = width // FEATS
    table = max(slots, n_row * own)
    vmem = pl.BlockSpec(memory_space=pltpu.VMEM)
    smem = pl.BlockSpec(memory_space=pltpu.SMEM)
    return pl.pallas_call(
        functools.partial(layer_kernel, n_row, n_col),
        out_shape=jax.ShapeDtypeStruct((own, width, lanes), jnp.float32),
        in_specs=[pl.BlockSpec(memory_space=pl.ANY)] * 3 + [vmem, vmem, smem],
        out_specs=vmem,
        scratch_shapes=[
            pltpu.VMEM((own, width, lanes), jnp.bfloat16),
            pltpu.VMEM((own, lanes), jnp.int32),
            pltpu.VMEM((8, table), jnp.int32),
            pltpu.VMEM((8, table), jnp.float32),
            pltpu.SMEM((8, table), jnp.int32),
            pltpu.SMEM((8, table), jnp.float32),
            pltpu.VMEM((slots, lanes, lanes), jnp.bfloat16),
            [pltpu.VMEM((n_col * own, FEATS, lanes), jnp.bfloat16) for _ in range(chunks)],
            pltpu.VMEM((chunks, n_row, own, FEATS, lanes), jnp.bfloat16),
            pltpu.VMEM((chunks, n_row, own, FEATS, lanes), jnp.bfloat16),
            pltpu.VMEM((slots // n_row, FEATS, lanes), jnp.float32),
            pltpu.SemaphoreType.DMA((PIECES,)),
            pltpu.SemaphoreType.DMA((4,)),
            pltpu.SemaphoreType.DMA((chunks, n_col)),
            pltpu.SemaphoreType.DMA((chunks, n_col)),
            pltpu.SemaphoreType.DMA((chunks,)),
            pltpu.SemaphoreType.DMA((chunks, n_row)),
            pltpu.SemaphoreType.DMA((chunks, n_row)),
        ],
        compiler_params=pltpu.CompilerParams(
            collective_id=0, has_side_effects=True, vmem_limit_bytes=48 * 1024 * 1024
        ),
    )(emb, degrees, tiles, rows, cols, count)


def shards(embedding, combined, blocks, block_rows, block_cols, block_counts, degrees):
    n_row = lax.axis_size("row")
    n_col = lax.axis_size("col")
    r = lax.axis_index("row")
    c = lax.axis_index("col")
    own, _, lanes = embedding.shape

    total = propagate(
        n_row,
        n_col,
        embedding,
        degrees.reshape(-1, lanes),
        blocks[0],
        block_rows,
        block_cols,
        block_counts,
    )
    part = lax.dynamic_slice_in_dim(degrees, (c * n_row + r) * own * lanes, own * lanes, 0)
    root = (1.0 / jnp.sqrt(part.astype(jnp.float32))).reshape(own, 1, lanes)
    update = total * root
    return update.astype(jnp.bfloat16), combined + update


def solution(mesh):
    return jax.shard_map(
        shards,
        mesh=mesh,
        in_specs=(
            P(("groups", "row", "col"), None, None),
            P(("groups", "col", "row"), None, None),
            P(("groups", "row", "col"), None, None, None),
            P(("groups", "row", "col"), None),
            P(("groups", "row", "col"), None),
            P(("groups", "row", "col")),
            P("groups"),
        ),
        out_specs=(
            P(("groups", "col", "row"), None, None),
            P(("groups", "col", "row"), None, None),
        ),
        check_vma=False,
    )
```

```python
import functools

import jax
import jax.numpy as jnp
from jax import lax
from jax.experimental import pallas as pl
from jax.experimental.pallas import tpu as pltpu
from jax.sharding import PartitionSpec as P

MESH = pl.DeviceIdType.MESH
FEATS = 16
PIECES = 4


def order_slots(n_row, own, rows_ref, cols_ref, count_ref, whole, real):
    slots = rows_ref.shape[1]
    dests = n_row * own
    per_share = slots // n_row
    shape = (slots, slots)
    down = lax.broadcasted_iota(jnp.int32, shape, 0)
    along = lax.broadcasted_iota(jnp.int32, shape, 1)
    both = cols_ref[...] * slots + rows_ref[...]
    both_down = jnp.sum(jnp.where(down == along, both, 0), axis=1, keepdims=True)
    cols = cols_ref[...]
    cols_down = both_down // slots
    earlier = cols * slots + along < cols_down * slots + down
    rank = jnp.sum(earlier.astype(jnp.int32), axis=1, keepdims=True)
    same = jnp.logical_and(earlier, cols == cols_down)
    repeats = (jnp.sum(same.astype(jnp.int32), axis=1, keepdims=True) > 0).astype(jnp.float32)
    hit = rank == along
    down_one = lax.broadcasted_iota(jnp.int32, (slots, 1), 0)
    alive = (down_one < count_ref[0]).astype(jnp.float32)

    def ordered(values):
        return jnp.sum(jnp.where(hit, values, jnp.zeros_like(values)), axis=0, keepdims=True)

    whole[0:1, 0:slots] = ordered(down_one)
    whole[1:2, 0:slots] = ordered(both_down - cols_down * slots)
    real[0:1, 0:slots] = ordered(repeats)
    real[1:2, 0:slots] = ordered(alive)
    dest = lax.broadcasted_iota(jnp.int32, (slots, dests), 1)
    upto = jnp.sum((cols_down <= dest).astype(jnp.int32), axis=0, keepdims=True)
    named = jnp.sum((cols_down == dest).astype(jnp.int32), axis=0, keepdims=True)
    dest_one = lax.broadcasted_iota(jnp.int32, (1, dests), 1)
    last = upto - 1 - dest_one // own * per_share
    whole[2:3, 0:dests] = jnp.clip(last, 0, per_share - 1)
    real[2:3, 0:dests] = (named > 0).astype(jnp.float32)


def layer_kernel(
    n_row,
    n_col,
    emb_hbm,
    degree_hbm,
    blocks_ref,
    rows_ref,
    cols_ref,
    count_ref,
    out_ref,
    emb_ref,
    degree_ref,
    whole_vmem,
    real_vmem,
    whole_smem,
    real_smem,
    tiles,
    gath,
    part,
    recv,
    running,
    blk_sem,
    in_sem,
    ag_send,
    ag_recv,
    fw_send,
    rs_send,
    rs_recv,
):
    own = emb_hbm.shape[0]
    chunks = emb_hbm.shape[1] // FEATS
    slots = blocks_ref.shape[0]
    per_share = slots // n_row
    piece = slots // PIECES
    g = lax.axis_index("groups")
    r = lax.axis_index("row")
    c = lax.axis_index("col")

    def block_copy(i):
        span = pl.ds(i * piece, piece)
        return pltpu.make_async_copy(blocks_ref.at[span], tiles.at[span], blk_sem.at[i])

    first = (r * n_col + c) * own
    emb_copy = pltpu.make_async_copy(emb_hbm, emb_ref, in_sem.at[0])
    degree_copy = pltpu.make_async_copy(degree_hbm.at[pl.ds(first, own)], degree_ref, in_sem.at[1])
    emb_copy.start()
    degree_copy.start()
    def row_peer(j):
        base = lax.rem(r + (j - j % 2), n_row)
        return base if j % 2 == 0 else base + 1 - 2 * lax.rem(base, 2)

    barrier = pltpu.get_barrier_semaphore()
    for d in range(1, n_col):
        pl.semaphore_signal(
            barrier, inc=1, device_id=(g, r, lax.rem(c + d, n_col)), device_id_type=MESH
        )
    for j in range(1, n_row):
        pl.semaphore_signal(barrier, inc=1, device_id=(g, row_peer(j), c), device_id_type=MESH)

    degree_copy.wait()
    emb_copy.wait()
    scale = (1.0 / jnp.sqrt(degree_ref[...].astype(jnp.float32)))[:, None, :]

    def scale_chunk(ch):
        feats = pl.ds(ch * FEATS, FEATS)
        gath[ch][pl.ds(c * own, own)] = (
            emb_ref[:, feats, :].astype(jnp.float32) * scale
        ).astype(jnp.bfloat16)

    scale_chunk(0)
    pl.semaphore_wait(barrier, n_col - 1 + n_row - 1)

    def shard_copy(ch, shard, send, target):
        span = gath[ch].at[pl.ds(shard * own, own)]
        return pltpu.make_async_remote_copy(
            src_ref=span,
            dst_ref=span,
            send_sem=send,
            recv_sem=ag_recv.at[ch, shard],
            device_id=(g, r, target),
            device_id_type=MESH,
        )

    line = n_col == 4
    if line:
        near = c + 1 - 2 * lax.rem(c, 2)
        far = lax.rem(c + 2, 4)
        across = 3 - c
        inner = jnp.logical_or(c == 1, c == 2)

    def start_own(ch):
        if line:
            shard_copy(ch, c, ag_send.at[ch, 0], far).start()
            shard_copy(ch, c, ag_send.at[ch, 1], near).start()

            @pl.when(inner)
            def _():
                shard_copy(ch, c, ag_send.at[ch, 2], across).start()
        else:
            for d in range(1, n_col):
                shard_copy(ch, c, ag_send.at[ch, d - 1], lax.rem(c + d, n_col)).start()

    def await_shards(ch):
        if line:
            shard_copy(ch, far, fw_send.at[ch], near).wait_recv()

            @pl.when(inner)
            def _():
                shard_copy(ch, far, fw_send.at[ch], near).start()

    def await_rest(ch):
        if line:
            shard_copy(ch, near, fw_send.at[ch], near).wait_recv()
            shard_copy(ch, across, fw_send.at[ch], near).wait_recv()
        else:
            for d in range(1, n_col):
                shard = lax.rem(c + d, n_col)
                shard_copy(ch, shard, ag_send.at[ch, 0], shard).wait_recv()

    def finish_sends(ch):
        if line:
            shard_copy(ch, c, ag_send.at[ch, 0], far).wait_send()
            shard_copy(ch, c, ag_send.at[ch, 1], near).wait_send()

            @pl.when(inner)
            def _():
                shard_copy(ch, c, ag_send.at[ch, 2], across).wait_send()
                shard_copy(ch, far, fw_send.at[ch], near).wait_send()
        else:
            for d in range(1, n_col):
                shard_copy(ch, c, ag_send.at[ch, d - 1], lax.rem(c + d, n_col)).wait_send()

    def sum_copy(ch, j):
        return pltpu.make_async_remote_copy(
            src_ref=part.at[ch, j],
            dst_ref=recv.at[ch, j],
            send_sem=rs_send.at[ch, j],
            recv_sem=rs_recv.at[ch, j],
            device_id=(g, row_peer(1 if j % 2 else j), c),
            device_id_type=MESH,
        )

    def share_sums(ch, share):
        base = share * per_share

        def slot(k, total):
            i = base + k
            x = gath[ch][whole_smem[1, i]]
            product = jnp.dot(x, tiles[whole_smem[0, i]], preferred_element_type=jnp.float32)
            total = total * real_smem[0, i] + product * real_smem[1, i]
            running[k] = total
            return total

        lax.fori_loop(
            0, per_share, slot, jnp.zeros((FEATS, running.shape[2]), jnp.float32), unroll=16
        )

    def compute(ch):
        pairs = [j for even in range(2, n_row, 2) for j in (even + 1, even)]
        for j in pairs + [1, 0]:
            share = row_peer(j)
            share_sums(ch, share)
            if j > 1 and j % 2 == 0:
                sum_copy(ch, j + 1).wait_recv()

            def place(d, carry):
                i = share * own + d
                value = running[whole_smem[2, i]] * real_smem[2, i]
                if j > 1 and j % 2 == 0:
                    value = value + recv[ch, j + 1, d].astype(jnp.float32)
                if j == 0:
                    out_ref[d, pl.ds(ch * FEATS, FEATS), :] = value
                else:
                    part[ch, j, d] = value.astype(jnp.bfloat16)
                return carry

            lax.fori_loop(0, own, place, 0, unroll=8)
            if j:
                sum_copy(ch, j).start()

    def reduce(ch):
        feats = pl.ds(ch * FEATS, FEATS)
        arrivals = [1] + list(range(2, n_row, 2))
        for j in arrivals:
            sum_copy(ch, j).wait_recv()
        value = out_ref[:, feats, :]
        for j in arrivals:
            value = value + recv[ch, j].astype(jnp.float32)
        out_ref[:, feats, :] = value

    start_own(0)
    scale_chunk(1)
    start_own(1)
    for i in range(PIECES):
        block_copy(i).start()
    for ch in range(2, chunks):
        scale_chunk(ch)
    order_slots(n_row, own, rows_ref, cols_ref, count_ref, whole_vmem, real_vmem)
    to_scalar = [
        pltpu.make_async_copy(whole_vmem, whole_smem, in_sem.at[2]),
        pltpu.make_async_copy(real_vmem, real_smem, in_sem.at[3]),
    ]
    for copy in to_scalar:
        copy.start()
    for copy in to_scalar:
        copy.wait()
    for i in range(PIECES):
        block_copy(i).wait()
    for ch in range(chunks):
        await_shards(ch)
        if ch + 2 < chunks:
            start_own(ch + 2)
        await_rest(ch)
        compute(ch)
        if ch:
            reduce(ch - 1)
    reduce(chunks - 1)
    for ch in range(chunks):
        finish_sends(ch)
        for j in range(1, n_row):
            sum_copy(ch, j).wait_send()


def propagate(n_row, n_col, emb, degrees, tiles, rows, cols, count):
    own, width, lanes = emb.shape
    slots = tiles.shape[0]
    chunks = width // FEATS
    table = max(slots, n_row * own)
    vmem = pl.BlockSpec(memory_space=pltpu.VMEM)
    smem = pl.BlockSpec(memory_space=pltpu.SMEM)
    return pl.pallas_call(
        functools.partial(layer_kernel, n_row, n_col),
        out_shape=jax.ShapeDtypeStruct((own, width, lanes), jnp.float32),
        in_specs=[pl.BlockSpec(memory_space=pl.ANY)] * 3 + [vmem, vmem, smem],
        out_specs=vmem,
        scratch_shapes=[
            pltpu.VMEM((own, width, lanes), jnp.bfloat16),
            pltpu.VMEM((own, lanes), jnp.int32),
            pltpu.VMEM((8, table), jnp.int32),
            pltpu.VMEM((8, table), jnp.float32),
            pltpu.SMEM((8, table), jnp.int32),
            pltpu.SMEM((8, table), jnp.float32),
            pltpu.VMEM((slots, lanes, lanes), jnp.bfloat16),
            [pltpu.VMEM((n_col * own, FEATS, lanes), jnp.bfloat16) for _ in range(chunks)],
            pltpu.VMEM((chunks, n_row, own, FEATS, lanes), jnp.bfloat16),
            pltpu.VMEM((chunks, n_row, own, FEATS, lanes), jnp.bfloat16),
            pltpu.VMEM((slots // n_row, FEATS, lanes), jnp.float32),
            pltpu.SemaphoreType.DMA((PIECES,)),
            pltpu.SemaphoreType.DMA((4,)),
            pltpu.SemaphoreType.DMA((chunks, n_col)),
            pltpu.SemaphoreType.DMA((chunks, n_col)),
            pltpu.SemaphoreType.DMA((chunks,)),
            pltpu.SemaphoreType.DMA((chunks, n_row)),
            pltpu.SemaphoreType.DMA((chunks, n_row)),
        ],
        compiler_params=pltpu.CompilerParams(
            collective_id=0, has_side_effects=True, vmem_limit_bytes=48 * 1024 * 1024
        ),
    )(emb, degrees, tiles, rows, cols, count)


def shards(embedding, combined, blocks, block_rows, block_cols, block_counts, degrees):
    n_row = lax.axis_size("row")
    n_col = lax.axis_size("col")
    r = lax.axis_index("row")
    c = lax.axis_index("col")
    own, _, lanes = embedding.shape

    total = propagate(
        n_row,
        n_col,
        embedding,
        degrees.reshape(-1, lanes),
        blocks[0],
        block_rows,
        block_cols,
        block_counts,
    )
    part = lax.dynamic_slice_in_dim(degrees, (c * n_row + r) * own * lanes, own * lanes, 0)
    root = (1.0 / jnp.sqrt(part.astype(jnp.float32))).reshape(own, 1, lanes)
    update = total * root
    return update.astype(jnp.bfloat16), combined + update


def solution(mesh):
    return jax.shard_map(
        shards,
        mesh=mesh,
        in_specs=(
            P(("groups", "row", "col"), None, None),
            P(("groups", "col", "row"), None, None),
            P(("groups", "row", "col"), None, None, None),
            P(("groups", "row", "col"), None),
            P(("groups", "row", "col"), None),
            P(("groups", "row", "col")),
            P("groups"),
        ),
        out_specs=(
            P(("groups", "col", "row"), None, None),
            P(("groups", "col", "row"), None, None),
        ),
        check_vma=False,
    )
```

```python
import functools

import jax
import jax.numpy as jnp
from jax import lax
from jax.experimental import pallas as pl
from jax.experimental.pallas import tpu as pltpu
from jax.sharding import PartitionSpec as P

MESH = pl.DeviceIdType.MESH
FEATS = 16
PIECES = 4


def order_slots(n_row, own, rows_ref, cols_ref, count_ref, whole, real):
    slots = rows_ref.shape[1]
    dests = n_row * own
    per_share = slots // n_row
    shape = (slots, slots)
    down = lax.broadcasted_iota(jnp.int32, shape, 0)
    along = lax.broadcasted_iota(jnp.int32, shape, 1)
    both = cols_ref[...] * slots + rows_ref[...]
    both_down = jnp.sum(jnp.where(down == along, both, 0), axis=1, keepdims=True)
    cols = cols_ref[...]
    cols_down = both_down // slots
    earlier = cols * slots + along < cols_down * slots + down
    rank = jnp.sum(earlier.astype(jnp.int32), axis=1, keepdims=True)
    same = jnp.logical_and(earlier, cols == cols_down)
    repeats = (jnp.sum(same.astype(jnp.int32), axis=1, keepdims=True) > 0).astype(jnp.float32)
    hit = rank == along
    down_one = lax.broadcasted_iota(jnp.int32, (slots, 1), 0)
    alive = (down_one < count_ref[0]).astype(jnp.float32)

    def ordered(values):
        return jnp.sum(jnp.where(hit, values, jnp.zeros_like(values)), axis=0, keepdims=True)

    whole[0:1, 0:slots] = ordered(down_one)
    whole[1:2, 0:slots] = ordered(both_down - cols_down * slots)
    real[0:1, 0:slots] = ordered(repeats)
    real[1:2, 0:slots] = ordered(alive)
    dest = lax.broadcasted_iota(jnp.int32, (slots, dests), 1)
    upto = jnp.sum((cols_down <= dest).astype(jnp.int32), axis=0, keepdims=True)
    named = jnp.sum((cols_down == dest).astype(jnp.int32), axis=0, keepdims=True)
    dest_one = lax.broadcasted_iota(jnp.int32, (1, dests), 1)
    last = upto - 1 - dest_one // own * per_share
    whole[2:3, 0:dests] = jnp.clip(last, 0, per_share - 1)
    real[2:3, 0:dests] = (named > 0).astype(jnp.float32)


def layer_kernel(
    n_row,
    n_col,
    emb_hbm,
    degree_hbm,
    blocks_ref,
    rows_ref,
    cols_ref,
    count_ref,
    out_ref,
    emb_ref,
    degree_ref,
    whole_vmem,
    real_vmem,
    whole_smem,
    real_smem,
    tiles,
    gath,
    part,
    recv,
    running,
    blk_sem,
    in_sem,
    ag_send,
    ag_recv,
    fw_send,
    rs_send,
    rs_recv,
):
    own = emb_hbm.shape[0]
    chunks = emb_hbm.shape[1] // FEATS
    slots = blocks_ref.shape[0]
    per_share = slots // n_row
    piece = slots // PIECES
    g = lax.axis_index("groups")
    r = lax.axis_index("row")
    c = lax.axis_index("col")

    def block_copy(i):
        span = pl.ds(i * piece, piece)
        return pltpu.make_async_copy(blocks_ref.at[span], tiles.at[span], blk_sem.at[i])

    first = (r * n_col + c) * own
    emb_copy = pltpu.make_async_copy(emb_hbm, emb_ref, in_sem.at[0])
    degree_copy = pltpu.make_async_copy(degree_hbm.at[pl.ds(first, own)], degree_ref, in_sem.at[1])
    emb_copy.start()
    degree_copy.start()
    for i in range(PIECES):
        block_copy(i).start()

    def row_peer(j):
        base = lax.rem(r + (j - j % 2), n_row)
        return base if j % 2 == 0 else base + 1 - 2 * lax.rem(base, 2)

    barrier = pltpu.get_barrier_semaphore()
    for d in range(1, n_col):
        pl.semaphore_signal(
            barrier, inc=1, device_id=(g, r, lax.rem(c + d, n_col)), device_id_type=MESH
        )
    for j in range(1, n_row):
        pl.semaphore_signal(barrier, inc=1, device_id=(g, row_peer(j), c), device_id_type=MESH)

    degree_copy.wait()
    emb_copy.wait()
    scale = (1.0 / jnp.sqrt(degree_ref[...].astype(jnp.float32)))[:, None, :]

    def scale_chunk(ch):
        feats = pl.ds(ch * FEATS, FEATS)
        gath[ch][pl.ds(c * own, own)] = (
            emb_ref[:, feats, :].astype(jnp.float32) * scale
        ).astype(jnp.bfloat16)

    for ch in range(chunks):
        scale_chunk(ch)
    pl.semaphore_wait(barrier, n_col - 1 + n_row - 1)

    def shard_copy(ch, shard, send, target):
        span = gath[ch].at[pl.ds(shard * own, own)]
        return pltpu.make_async_remote_copy(
            src_ref=span,
            dst_ref=span,
            send_sem=send,
            recv_sem=ag_recv.at[ch, shard],
            device_id=(g, r, target),
            device_id_type=MESH,
        )

    line = n_col == 4
    if line:
        near = c + 1 - 2 * lax.rem(c, 2)
        far = lax.rem(c + 2, 4)
        across = 3 - c
        inner = jnp.logical_or(c == 1, c == 2)

    def start_own(ch):
        if line:
            shard_copy(ch, c, ag_send.at[ch, 0], far).start()
            shard_copy(ch, c, ag_send.at[ch, 1], near).start()

            @pl.when(inner)
            def _():
                shard_copy(ch, c, ag_send.at[ch, 2], across).start()
        else:
            for d in range(1, n_col):
                shard_copy(ch, c, ag_send.at[ch, d - 1], lax.rem(c + d, n_col)).start()

    def await_shards(ch):
        if line:
            shard_copy(ch, far, fw_send.at[ch], near).wait_recv()

            @pl.when(inner)
            def _():
                shard_copy(ch, far, fw_send.at[ch], near).start()

    def await_rest(ch):
        if line:
            shard_copy(ch, near, fw_send.at[ch], near).wait_recv()
            shard_copy(ch, across, fw_send.at[ch], near).wait_recv()
        else:
            for d in range(1, n_col):
                shard = lax.rem(c + d, n_col)
                shard_copy(ch, shard, ag_send.at[ch, 0], shard).wait_recv()

    def finish_sends(ch):
        if line:
            shard_copy(ch, c, ag_send.at[ch, 0], far).wait_send()
            shard_copy(ch, c, ag_send.at[ch, 1], near).wait_send()

            @pl.when(inner)
            def _():
                shard_copy(ch, c, ag_send.at[ch, 2], across).wait_send()
                shard_copy(ch, far, fw_send.at[ch], near).wait_send()
        else:
            for d in range(1, n_col):
                shard_copy(ch, c, ag_send.at[ch, d - 1], lax.rem(c + d, n_col)).wait_send()

    def sum_copy(ch, j):
        return pltpu.make_async_remote_copy(
            src_ref=part.at[ch, j],
            dst_ref=recv.at[ch, j],
            send_sem=rs_send.at[ch, j],
            recv_sem=rs_recv.at[ch, j],
            device_id=(g, row_peer(j), c),
            device_id_type=MESH,
        )

    def share_sums(ch, share):
        base = share * per_share

        def slot(k, total):
            i = base + k
            x = gath[ch][whole_smem[1, i]]
            product = jnp.dot(x, tiles[whole_smem[0, i]], preferred_element_type=jnp.float32)
            total = total * real_smem[0, i] + product * real_smem[1, i]
            running[k] = total
            return total

        lax.fori_loop(
            0, per_share, slot, jnp.zeros((FEATS, running.shape[2]), jnp.float32), unroll=min(64, per_share)
        )

    def compute(ch):
        for j in list(range(2, n_row)) + [1, 0]:
            share = row_peer(j)
            share_sums(ch, share)

            def place(d, carry):
                i = share * own + d
                value = running[whole_smem[2, i]] * real_smem[2, i]
                if j == 0:
                    out_ref[d, pl.ds(ch * FEATS, FEATS), :] = value
                else:
                    part[ch, j, d] = value.astype(jnp.bfloat16)
                return carry

            lax.fori_loop(0, own, place, 0, unroll=32)
            if j:
                sum_copy(ch, j).start()

    def reduce(ch):
        feats = pl.ds(ch * FEATS, FEATS)
        for j in range(1, n_row):
            sum_copy(ch, j).wait_recv()
        value = out_ref[:, feats, :]
        for j in range(1, n_row):
            value = value + recv[ch, j].astype(jnp.float32)
        out_ref[:, feats, :] = value

    start_own(0)
    start_own(1)
    order_slots(n_row, own, rows_ref, cols_ref, count_ref, whole_vmem, real_vmem)
    to_scalar = [
        pltpu.make_async_copy(whole_vmem, whole_smem, in_sem.at[2]),
        pltpu.make_async_copy(real_vmem, real_smem, in_sem.at[3]),
    ]
    for copy in to_scalar:
        copy.start()
    for copy in to_scalar:
        copy.wait()
    for i in range(PIECES):
        block_copy(i).wait()
    for ch in range(chunks):
        await_shards(ch)
        if ch + 2 < chunks:
            start_own(ch + 2)
        await_rest(ch)
        compute(ch)
        if ch:
            reduce(ch - 1)
    reduce(chunks - 1)
    for ch in range(chunks):
        finish_sends(ch)
        for j in range(1, n_row):
            sum_copy(ch, j).wait_send()


def propagate(n_row, n_col, emb, degrees, tiles, rows, cols, count):
    own, width, lanes = emb.shape
    slots = tiles.shape[0]
    chunks = width // FEATS
    table = max(slots, n_row * own)
    vmem = pl.BlockSpec(memory_space=pltpu.VMEM)
    smem = pl.BlockSpec(memory_space=pltpu.SMEM)
    return pl.pallas_call(
        functools.partial(layer_kernel, n_row, n_col),
        out_shape=jax.ShapeDtypeStruct((own, width, lanes), jnp.float32),
        in_specs=[pl.BlockSpec(memory_space=pl.ANY)] * 3 + [vmem, vmem, smem],
        out_specs=vmem,
        scratch_shapes=[
            pltpu.VMEM((own, width, lanes), jnp.bfloat16),
            pltpu.VMEM((own, lanes), jnp.int32),
            pltpu.VMEM((8, table), jnp.int32),
            pltpu.VMEM((8, table), jnp.float32),
            pltpu.SMEM((8, table), jnp.int32),
            pltpu.SMEM((8, table), jnp.float32),
            pltpu.VMEM((slots, lanes, lanes), jnp.bfloat16),
            [pltpu.VMEM((n_col * own, FEATS, lanes), jnp.bfloat16) for _ in range(chunks)],
            pltpu.VMEM((chunks, n_row, own, FEATS, lanes), jnp.bfloat16),
            pltpu.VMEM((chunks, n_row, own, FEATS, lanes), jnp.bfloat16),
            pltpu.VMEM((slots // n_row, FEATS, lanes), jnp.float32),
            pltpu.SemaphoreType.DMA((PIECES,)),
            pltpu.SemaphoreType.DMA((4,)),
            pltpu.SemaphoreType.DMA((chunks, n_col)),
            pltpu.SemaphoreType.DMA((chunks, n_col)),
            pltpu.SemaphoreType.DMA((chunks,)),
            pltpu.SemaphoreType.DMA((chunks, n_row)),
            pltpu.SemaphoreType.DMA((chunks, n_row)),
        ],
        compiler_params=pltpu.CompilerParams(
            collective_id=0, has_side_effects=True, vmem_limit_bytes=48 * 1024 * 1024
        ),
    )(emb, degrees, tiles, rows, cols, count)


def shards(embedding, combined, blocks, block_rows, block_cols, block_counts, degrees):
    n_row = lax.axis_size("row")
    n_col = lax.axis_size("col")
    r = lax.axis_index("row")
    c = lax.axis_index("col")
    own, _, lanes = embedding.shape

    total = propagate(
        n_row,
        n_col,
        embedding,
        degrees.reshape(-1, lanes),
        blocks[0],
        block_rows,
        block_cols,
        block_counts,
    )
    part = lax.dynamic_slice_in_dim(degrees, (c * n_row + r) * own * lanes, own * lanes, 0)
    root = (1.0 / jnp.sqrt(part.astype(jnp.float32))).reshape(own, 1, lanes)
    update = total * root
    return update.astype(jnp.bfloat16), combined + update


def solution(mesh):
    return jax.shard_map(
        shards,
        mesh=mesh,
        in_specs=(
            P(("groups", "row", "col"), None, None),
            P(("groups", "col", "row"), None, None),
            P(("groups", "row", "col"), None, None, None),
            P(("groups", "row", "col"), None),
            P(("groups", "row", "col"), None),
            P(("groups", "row", "col")),
            P("groups"),
        ),
        out_specs=(
            P(("groups", "col", "row"), None, None),
            P(("groups", "col", "row"), None, None),
        ),
        check_vma=False,
    )
```

```python
import functools

import jax
import jax.numpy as jnp
from jax import lax
from jax.experimental import pallas as pl
from jax.experimental.pallas import tpu as pltpu
from jax.sharding import PartitionSpec as P

MESH = pl.DeviceIdType.MESH
FEATS = 16
PIECES = 4


def order_slots(n_row, own, rows_ref, cols_ref, count_ref, whole, real):
    slots = rows_ref.shape[1]
    dests = n_row * own
    per_share = slots // n_row
    shape = (slots, slots)
    down = lax.broadcasted_iota(jnp.int32, shape, 0)
    along = lax.broadcasted_iota(jnp.int32, shape, 1)
    both = cols_ref[...] * slots + rows_ref[...]
    both_down = jnp.sum(jnp.where(down == along, both, 0), axis=1, keepdims=True)
    cols = cols_ref[...]
    cols_down = both_down // slots
    earlier = cols * slots + along < cols_down * slots + down
    rank = jnp.sum(earlier.astype(jnp.int32), axis=1, keepdims=True)
    same = jnp.logical_and(earlier, cols == cols_down)
    repeats = (jnp.sum(same.astype(jnp.int32), axis=1, keepdims=True) > 0).astype(jnp.float32)
    hit = rank == along
    down_one = lax.broadcasted_iota(jnp.int32, (slots, 1), 0)
    alive = (down_one < count_ref[0]).astype(jnp.float32)

    def ordered(values):
        return jnp.sum(jnp.where(hit, values, jnp.zeros_like(values)), axis=0, keepdims=True)

    whole[0:1, 0:slots] = ordered(down_one)
    whole[1:2, 0:slots] = ordered(both_down - cols_down * slots)
    real[0:1, 0:slots] = ordered(repeats)
    real[1:2, 0:slots] = ordered(alive)
    dest = lax.broadcasted_iota(jnp.int32, (slots, dests), 1)
    upto = jnp.sum((cols_down <= dest).astype(jnp.int32), axis=0, keepdims=True)
    named = jnp.sum((cols_down == dest).astype(jnp.int32), axis=0, keepdims=True)
    dest_one = lax.broadcasted_iota(jnp.int32, (1, dests), 1)
    last = upto - 1 - dest_one // own * per_share
    whole[2:3, 0:dests] = jnp.clip(last, 0, per_share - 1)
    real[2:3, 0:dests] = (named > 0).astype(jnp.float32)


def layer_kernel(
    n_row,
    n_col,
    emb_hbm,
    degree_hbm,
    blocks_ref,
    rows_ref,
    cols_ref,
    count_ref,
    out_ref,
    emb_ref,
    degree_ref,
    whole_vmem,
    real_vmem,
    whole_smem,
    real_smem,
    tiles,
    gath,
    part,
    recv,
    running,
    blk_sem,
    in_sem,
    ag_send,
    ag_recv,
    fw_send,
    rs_send,
    rs_recv,
):
    own = emb_hbm.shape[0]
    chunks = emb_hbm.shape[1] // FEATS
    slots = blocks_ref.shape[0]
    per_share = slots // n_row
    piece = slots // PIECES
    g = lax.axis_index("groups")
    r = lax.axis_index("row")
    c = lax.axis_index("col")

    def block_copy(i):
        span = pl.ds(i * piece, piece)
        return pltpu.make_async_copy(blocks_ref.at[span], tiles.at[span], blk_sem.at[i])

    first = (r * n_col + c) * own
    emb_copy = pltpu.make_async_copy(emb_hbm, emb_ref, in_sem.at[0])
    degree_copy = pltpu.make_async_copy(degree_hbm.at[pl.ds(first, own)], degree_ref, in_sem.at[1])
    emb_copy.start()
    degree_copy.start()
    for i in range(PIECES):
        block_copy(i).start()

    def row_peer(j):
        base = lax.rem(r + (j - j % 2), n_row)
        return base if j % 2 == 0 else base + 1 - 2 * lax.rem(base, 2)

    barrier = pltpu.get_barrier_semaphore()
    for d in range(1, n_col):
        pl.semaphore_signal(
            barrier, inc=1, device_id=(g, r, lax.rem(c + d, n_col)), device_id_type=MESH
        )
    for j in range(1, n_row):
        pl.semaphore_signal(barrier, inc=1, device_id=(g, row_peer(j), c), device_id_type=MESH)

    degree_copy.wait()
    emb_copy.wait()
    scale = (1.0 / jnp.sqrt(degree_ref[...].astype(jnp.float32)))[:, None, :]

    def scale_chunk(ch):
        feats = pl.ds(ch * FEATS, FEATS)
        gath[ch][pl.ds(c * own, own)] = (
            emb_ref[:, feats, :].astype(jnp.float32) * scale
        ).astype(jnp.bfloat16)

    scale_chunk(0)
    pl.semaphore_wait(barrier, n_col - 1 + n_row - 1)

    def shard_copy(ch, shard, send, target):
        span = gath[ch].at[pl.ds(shard * own, own)]
        return pltpu.make_async_remote_copy(
            src_ref=span,
            dst_ref=span,
            send_sem=send,
            recv_sem=ag_recv.at[ch, shard],
            device_id=(g, r, target),
            device_id_type=MESH,
        )

    line = n_col == 4
    if line:
        near = c + 1 - 2 * lax.rem(c, 2)
        far = lax.rem(c + 2, 4)
        across = 3 - c
        inner = jnp.logical_or(c == 1, c == 2)

    def start_own(ch):
        if line:
            shard_copy(ch, c, ag_send.at[ch, 0], far).start()
            shard_copy(ch, c, ag_send.at[ch, 1], near).start()

            @pl.when(inner)
            def _():
                shard_copy(ch, c, ag_send.at[ch, 2], across).start()
        else:
            for d in range(1, n_col):
                shard_copy(ch, c, ag_send.at[ch, d - 1], lax.rem(c + d, n_col)).start()

    def forward(ch):
        if line:

            @pl.when(inner)
            def _():
                shard_copy(ch, far, fw_send.at[ch], near).wait_recv()
                shard_copy(ch, far, fw_send.at[ch], near).start()

    def await_rest(ch):
        if line:

            @pl.when(jnp.logical_not(inner))
            def _():
                shard_copy(ch, far, fw_send.at[ch], near).wait_recv()

            shard_copy(ch, near, fw_send.at[ch], near).wait_recv()
            shard_copy(ch, across, fw_send.at[ch], near).wait_recv()
        else:
            for d in range(1, n_col):
                shard = lax.rem(c + d, n_col)
                shard_copy(ch, shard, ag_send.at[ch, 0], shard).wait_recv()

    def finish_sends(ch):
        if line:
            shard_copy(ch, c, ag_send.at[ch, 0], far).wait_send()
            shard_copy(ch, c, ag_send.at[ch, 1], near).wait_send()

            @pl.when(inner)
            def _():
                shard_copy(ch, c, ag_send.at[ch, 2], across).wait_send()
                shard_copy(ch, far, fw_send.at[ch], near).wait_send()
        else:
            for d in range(1, n_col):
                shard_copy(ch, c, ag_send.at[ch, d - 1], lax.rem(c + d, n_col)).wait_send()

    def sum_copy(ch, j):
        return pltpu.make_async_remote_copy(
            src_ref=part.at[ch, j],
            dst_ref=recv.at[ch, j],
            send_sem=rs_send.at[ch, j],
            recv_sem=rs_recv.at[ch, j],
            device_id=(g, row_peer(j), c),
            device_id_type=MESH,
        )

    def share_sums(ch, share):
        base = share * per_share

        def slot(k, total):
            i = base + k
            x = gath[ch][whole_smem[1, i]]
            product = jnp.dot(x, tiles[whole_smem[0, i]], preferred_element_type=jnp.float32)
            total = total * real_smem[0, i] + product * real_smem[1, i]
            running[k] = total
            return total

        lax.fori_loop(
            0, per_share, slot, jnp.zeros((FEATS, running.shape[2]), jnp.float32), unroll=min(64, per_share)
        )

    def compute(ch):
        for j in list(range(2, n_row)) + [1, 0]:
            share = row_peer(j)
            share_sums(ch, share)

            def place(d, carry):
                i = share * own + d
                value = running[whole_smem[2, i]] * real_smem[2, i]
                if j == 0:
                    out_ref[d, pl.ds(ch * FEATS, FEATS), :] = value
                else:
                    part[ch, j, d] = value.astype(jnp.bfloat16)
                return carry

            lax.fori_loop(0, own, place, 0, unroll=32)
            if j:
                sum_copy(ch, j).start()

    def reduce(ch):
        feats = pl.ds(ch * FEATS, FEATS)
        for j in range(1, n_row):
            sum_copy(ch, j).wait_recv()
        value = out_ref[:, feats, :]
        for j in range(1, n_row):
            value = value + recv[ch, j].astype(jnp.float32)
        out_ref[:, feats, :] = value

    start_own(0)
    scale_chunk(1)
    start_own(1)
    for ch in range(2, chunks):
        scale_chunk(ch)
    order_slots(n_row, own, rows_ref, cols_ref, count_ref, whole_vmem, real_vmem)
    to_scalar = [
        pltpu.make_async_copy(whole_vmem, whole_smem, in_sem.at[2]),
        pltpu.make_async_copy(real_vmem, real_smem, in_sem.at[3]),
    ]
    for copy in to_scalar:
        copy.start()
    for copy in to_scalar:
        copy.wait()
    for i in range(PIECES):
        block_copy(i).wait()
    forward(0)
    for ch in range(chunks):
        if ch + 2 < chunks:
            start_own(ch + 2)
        if ch + 1 < chunks:
            forward(ch + 1)
        await_rest(ch)
        compute(ch)
        if ch:
            reduce(ch - 1)
    reduce(chunks - 1)
    for ch in range(chunks):
        finish_sends(ch)
        for j in range(1, n_row):
            sum_copy(ch, j).wait_send()


def propagate(n_row, n_col, emb, degrees, tiles, rows, cols, count):
    own, width, lanes = emb.shape
    slots = tiles.shape[0]
    chunks = width // FEATS
    table = max(slots, n_row * own)
    vmem = pl.BlockSpec(memory_space=pltpu.VMEM)
    smem = pl.BlockSpec(memory_space=pltpu.SMEM)
    return pl.pallas_call(
        functools.partial(layer_kernel, n_row, n_col),
        out_shape=jax.ShapeDtypeStruct((own, width, lanes), jnp.float32),
        in_specs=[pl.BlockSpec(memory_space=pl.ANY)] * 3 + [vmem, vmem, smem],
        out_specs=vmem,
        scratch_shapes=[
            pltpu.VMEM((own, width, lanes), jnp.bfloat16),
            pltpu.VMEM((own, lanes), jnp.int32),
            pltpu.VMEM((8, table), jnp.int32),
            pltpu.VMEM((8, table), jnp.float32),
            pltpu.SMEM((8, table), jnp.int32),
            pltpu.SMEM((8, table), jnp.float32),
            pltpu.VMEM((slots, lanes, lanes), jnp.bfloat16),
            [pltpu.VMEM((n_col * own, FEATS, lanes), jnp.bfloat16) for _ in range(chunks)],
            pltpu.VMEM((chunks, n_row, own, FEATS, lanes), jnp.bfloat16),
            pltpu.VMEM((chunks, n_row, own, FEATS, lanes), jnp.bfloat16),
            pltpu.VMEM((slots // n_row, FEATS, lanes), jnp.float32),
            pltpu.SemaphoreType.DMA((PIECES,)),
            pltpu.SemaphoreType.DMA((4,)),
            pltpu.SemaphoreType.DMA((chunks, n_col)),
            pltpu.SemaphoreType.DMA((chunks, n_col)),
            pltpu.SemaphoreType.DMA((chunks,)),
            pltpu.SemaphoreType.DMA((chunks, n_row)),
            pltpu.SemaphoreType.DMA((chunks, n_row)),
        ],
        compiler_params=pltpu.CompilerParams(
            collective_id=0, has_side_effects=True, vmem_limit_bytes=48 * 1024 * 1024
        ),
    )(emb, degrees, tiles, rows, cols, count)


def shards(embedding, combined, blocks, block_rows, block_cols, block_counts, degrees):
    n_row = lax.axis_size("row")
    n_col = lax.axis_size("col")
    r = lax.axis_index("row")
    c = lax.axis_index("col")
    own, _, lanes = embedding.shape

    total = propagate(
        n_row,
        n_col,
        embedding,
        degrees.reshape(-1, lanes),
        blocks[0],
        block_rows,
        block_cols,
        block_counts,
    )
    part = lax.dynamic_slice_in_dim(degrees, (c * n_row + r) * own * lanes, own * lanes, 0)
    root = (1.0 / jnp.sqrt(part.astype(jnp.float32))).reshape(own, 1, lanes)
    update = total * root
    return update.astype(jnp.bfloat16), combined + update


def solution(mesh):
    return jax.shard_map(
        shards,
        mesh=mesh,
        in_specs=(
            P(("groups", "row", "col"), None, None),
            P(("groups", "col", "row"), None, None),
            P(("groups", "row", "col"), None, None, None),
            P(("groups", "row", "col"), None),
            P(("groups", "row", "col"), None),
            P(("groups", "row", "col")),
            P("groups"),
        ),
        out_specs=(
            P(("groups", "col", "row"), None, None),
            P(("groups", "col", "row"), None, None),
        ),
        check_vma=False,
    )
```
